256 devices in a mesh: gx: 32 (over x, y, z_hi), gy: 8 (over z_lo, core).
Axes of the slice: x: 4, y: 4, z: 8 (z_hi: 2, z_lo: 4; z = z_hi * 4 + z_lo), core: 2. Of those that a mesh axis runs over, the one named last changes fastest.
Arguments:
- scalars: bfloat16 [32, 8, 256, 2048], P('gx', 'gy'), may hold values from -6 to 6
- tensors: bfloat16 [32, 8, 9, 64, 2048], P('gx', 'gy'), may hold values from -6 to 6
- vectors: float32 [32, 8, 3, 2048], P('gx', 'gy'), may hold values from -1 to 1
- species: int32 [32, 8, 2048], P('gx', 'gy'), may hold values from 0 to 3
- species_table: float32 [256, 4], replicated, may hold values from -3 to 3
- reverse: int32 [32, 8, 2048], P('gx', 'gy'), may hold values from 0 to 2559, as said below
- send_index: int32 [32, 8, 8, 64], P('gx', 'gy'), may hold values from 0 to 2047, as said below
- counts: int32 [32, 8, 8], P('gx', 'gy'), may hold values from 32 to 64, as said below
- w_query: bfloat16 [256, 256], replicated, may hold values from -0.375 to 0.375
- w_key: bfloat16 [256, 256], replicated, may hold values from -0.375 to 0.375
- w_value: bfloat16 [256, 256], replicated, may hold values from -0.375 to 0.375
- w_output: bfloat16 [256, 256], replicated, may hold values from -0.375 to 0.375
- w_invariant: bfloat16 [256, 192], replicated, may hold values from -0.4375 to 0.4375
- w_message: bfloat16 [256, 256], replicated, may hold values from -0.375 to 0.375
- w_gate: bfloat16 [192, 256], replicated, may hold values from -0.375 to 0.375
- w_radial: bfloat16 [192, 256], replicated, may hold values from -0.375 to 0.375
- w_mixing: bfloat16 [64, 64], replicated, may hold values from -0.75 to 0.75
- w_expand: bfloat16 [512, 256], replicated, may hold values from -0.375 to 0.375
- w_reverse: bfloat16 [512, 256], replicated, may hold values from -0.375 to 0.375
- w_contract: bfloat16 [256, 512], replicated, may hold values from -0.25 to 0.25
Outputs:
- new_scalars: bfloat16 [32, 8, 256, 2048], P('gx', 'gy')
- new_tensors: bfloat16 [32, 8, 9, 64, 2048], P('gx', 'gy')
The draws below stay inside these ranges and needn't reach their ends.
Inputs may be any that keep to these rules, and one draw needn't show every extreme that they name: counts[p] of a domain equals the count of its partner in direction p toward it (the opposite direction); some domain has 64 live slots toward some partner in every direction. `send_index`: live slots of a domain name distinct edges; slots at or above the count hold 0. The edge in live slot s of block p has as reverse slot s of the block received in the opposite direction; every live received slot is named by exactly one edge, no empty slot is named, and the other edges are paired among themselves (at most one edge of a domain is its own reverse).
All inputs are finite; a program needn't handle non-finite values.
Results may differ from the reference program's by a relative error of at most 0.01.
Values may be sent and summed in bfloat16 or wider, within the bound.
A program may use at most 64 MiB of HBM per device.

```python
import math
import jax
import jax.numpy as jnp
from jax import lax

C = 256
MUL = 64
FFN = 512
HEADS = 8
E_DEV = 2048
BLOCK = 64
DOM_X = 32
DOM_Y = 8


def boundary_plan(key):
    base = jax.random.fold_in(key, 11)
    key_count, key_perm = jax.random.split(base)
    halves = jax.random.randint(key_count, (DOM_X, DOM_Y, 4), BLOCK // 2, BLOCK + 1).astype(jnp.int32)
    halves = halves.at[0, 0, :].set(BLOCK)
    forward_ids = (0, 2, 4, 5)
    opposite_ids = (1, 3, 7, 6)
    steps_list = ((1, 0), (0, 1), (1, 1), (1, -1))
    columns = [None] * 8
    for number in range(4):
        step_x, step_y = steps_list[number]
        columns[forward_ids[number]] = halves[..., number]
        columns[opposite_ids[number]] = jnp.roll(halves[..., number], (step_x, step_y), axis=(0, 1))
    counts = jnp.stack(columns, axis=-1).astype(jnp.int32)
    keys = jax.random.split(key_perm, DOM_X * DOM_Y)
    perms = jax.vmap(lambda single: jax.random.permutation(single, E_DEV))(keys).astype(jnp.int32).reshape(DOM_X, DOM_Y, E_DEV)
    ends = jnp.cumsum(counts, axis=-1).astype(jnp.int32)
    starts = ends - counts
    slot_ids = jnp.arange(BLOCK, dtype=jnp.int32)
    positions = starts[..., None] + slot_ids
    live_slots = slot_ids < counts[..., None]
    picked = jnp.take_along_axis(perms, positions.reshape(DOM_X, DOM_Y, 8 * BLOCK), axis=-1).reshape(DOM_X, DOM_Y, 8, BLOCK)
    send_index = jnp.where(live_slots, picked, 0).astype(jnp.int32)
    ranks = jnp.arange(E_DEV, dtype=jnp.int32)
    total = ends[..., 7:8]
    rest = ranks - total
    partner_rank = total + rest + 1 - 2 * (rest % 2)
    partner_rank = jnp.where(partner_rank >= E_DEV, ranks, partner_rank)
    partner_rank = jnp.clip(partner_rank, 0, E_DEV - 1).astype(jnp.int32)
    interior_rev = jnp.take_along_axis(perms, partner_rank, axis=-1)
    direction = jnp.minimum(jnp.sum((ranks[..., None] >= ends[..., None, :]).astype(jnp.int32), axis=-1), 7).astype(jnp.int32)
    opposite_table = jnp.array([1, 0, 3, 2, 7, 6, 5, 4], dtype=jnp.int32)
    opposite = opposite_table[direction]
    within = ranks - jnp.take_along_axis(starts, direction, axis=-1)
    boundary_rev = E_DEV + opposite * BLOCK + within
    chosen = jnp.where(ranks < total, boundary_rev, interior_rev).astype(jnp.int32)
    flat_perm = perms.reshape(DOM_X * DOM_Y, E_DEV)
    flat_chosen = chosen.reshape(DOM_X * DOM_Y, E_DEV)
    reverse = jax.vmap(lambda order_ids, entries: jnp.zeros((E_DEV,), jnp.int32).at[order_ids].set(entries))(flat_perm, flat_chosen)
    return (counts, send_index, reverse.reshape(DOM_X, DOM_Y, E_DEV).astype(jnp.int32))


def draw_counts(key, part):
    return boundary_plan(key)[0]


def draw_send_index(key, part):
    return boundary_plan(key)[1]


def draw_reverse(key, part):
    return boundary_plan(key)[2]


def touch_ends(drawn, own_key, least, largest):
    extent = drawn.shape
    place = [jax.random.randint(jax.random.fold_in(own_key, axis), (), 0, extent[axis]) for axis in range(len(extent))]
    drawn = drawn.at[tuple(place)].set(least)
    longest = extent.index(max(extent))
    place[longest] = (place[longest] + 1) % extent[longest]
    return drawn.at[tuple(place)].set(largest)


def block_scale(stream_key, extent, pieces, low, high):
    def one(axis_at, shards_of):
        heights = jax.random.uniform(jax.random.fold_in(jax.random.fold_in(stream_key, 6), axis_at), (shards_of,), jnp.float32, low / len(pieces), high / len(pieces))
        return jnp.repeat(jnp.exp(heights), extent[axis_at] // shards_of).reshape((-1,) + (1,) * (len(extent) - axis_at - 1))

    loudness = one(*pieces[0])
    for cut in pieces[1:]:
        loudness = loudness * one(*cut)
    return loudness


def normal_values(rng, extent, scale, most, pieces=(), kind=jnp.bfloat16):
    values = jax.random.normal(rng, extent, jnp.float32) * scale
    if len(pieces) > 0:
        values = block_scale(rng, extent, pieces, -0.22, 0.18) * values
    return jnp.clip(values, min=-most, max=most).astype(kind)


def setup_inputs(seed: int = 0) -> dict:
    key_list = jax.random.split(jax.random.key(seed), 21)
    return {
        "scalars": normal_values(key_list[0], (DOM_X, DOM_Y, C, E_DEV), 1.0, 6.0, ((0, 32), (1, 8))),
        "tensors": normal_values(key_list[1], (DOM_X, DOM_Y, 9, MUL, E_DEV), 1.0, 6.0, ((0, 32), (1, 8))),
        "vectors": jnp.clip(jax.random.uniform(key_list[2], (DOM_X, DOM_Y, 3, E_DEV), jnp.float32, -1.0, 1.0) * block_scale(key_list[2], (DOM_X, DOM_Y, 3, E_DEV), ((0, 32), (1, 8)), -0.4, 0.0), -1.0, 1.0),
        "species": touch_ends(jax.random.randint(key_list[3], (DOM_X, DOM_Y, E_DEV), 0, 4), jax.random.fold_in(key_list[3], 1), 0, 3).astype(jnp.int32),
        "species_table": normal_values(key_list[4], (C, 4), 0.5, 3.0, (), jnp.float32),
        "reverse": draw_reverse(jax.random.fold_in(key_list[20], 71), 0),
        "send_index": draw_send_index(jax.random.fold_in(key_list[20], 71), 0),
        "counts": draw_counts(jax.random.fold_in(key_list[20], 71), 0),
        "w_query": normal_values(key_list[8], (C, C), C ** -0.5, 0.375),
        "w_key": normal_values(key_list[9], (C, C), C ** -0.5, 0.375),
        "w_value": normal_values(key_list[10], (C, C), C ** -0.5, 0.375),
        "w_output": normal_values(key_list[11], (C, C), C ** -0.5, 0.375),
        "w_invariant": normal_values(key_list[12], (C, 3 * MUL), (3 * MUL) ** -0.5, 0.4375),
        "w_message": normal_values(key_list[13], (C, C), C ** -0.5, 0.375),
        "w_gate": normal_values(key_list[14], (3 * MUL, C), C ** -0.5, 0.375),
        "w_radial": normal_values(key_list[15], (3 * MUL, C), C ** -0.5, 0.375),
        "w_mixing": normal_values(key_list[16], (MUL, MUL), MUL ** -0.5, 0.75),
        "w_expand": normal_values(key_list[17], (FFN, C), C ** -0.5, 0.375),
        "w_reverse": normal_values(key_list[18], (FFN, C), C ** -0.5, 0.375),
        "w_contract": normal_values(key_list[19], (C, FFN), FFN ** -0.5, 0.25),
    }


DIRECTIONS = ((1, 0), (-1, 0), (0, 1), (0, -1), (1, 1), (1, -1), (-1, 1), (-1, -1))

def solid_harmonics(vectors):
    xcoord, ycoord, zcoord = (vectors[0], vectors[1], vectors[2])
    radius_sq = xcoord * xcoord + ycoord * ycoord + zcoord * zcoord
    root_three = math.sqrt(3.0)
    return jnp.stack([jnp.ones_like(xcoord), xcoord, ycoord, zcoord, root_three * xcoord * ycoord, root_three * ycoord * zcoord, 0.5 * (3.0 * zcoord * zcoord - radius_sq), root_three * xcoord * zcoord, 0.5 * root_three * (xcoord * xcoord - ycoord * ycoord)])

def by_degree(rows):
    multiplicity, edge_count = (rows.shape[1], rows.shape[2])
    return jnp.concatenate([rows[0:1], jnp.broadcast_to(rows[1:2], (3, multiplicity, edge_count)), jnp.broadcast_to(rows[2:3], (5, multiplicity, edge_count))], axis=0)

def send_blocks(scalars, tensors, send_index, counts):
    edge_count = scalars.shape[1]
    flatten = send_index.reshape(-1)
    picked = jnp.concatenate([jnp.take(scalars, flatten, axis=1), jnp.take(tensors.reshape(-1, edge_count), flatten, axis=1)], axis=0)
    live_slots = (lax.broadcasted_iota(jnp.int32, send_index.shape, 1) < counts[:, None]).reshape(-1)
    return jnp.where(live_slots[None, :], picked, jnp.zeros_like(picked))

def edge_update(scalars, tensors, vectors, species, reverse, received, species_table, weights):
    w_query, w_key, w_value, w_output, w_invariant, w_message, w_gate, w_radial, w_mixing = weights
    channels, edge_count = scalars.shape
    multiplicity = tensors.shape[1]
    table_scalar = jnp.concatenate([scalars, received[:channels]], axis=1)
    table_tensor = jnp.concatenate([tensors.reshape(9 * multiplicity, edge_count), received[channels:]], axis=1)
    scalar_rev = jnp.take(table_scalar, reverse, axis=1)
    tensor_rev = jnp.take(table_tensor, reverse, axis=1).reshape(9, multiplicity, edge_count)
    species_ids = lax.broadcasted_iota(jnp.int32, (species_table.shape[1], edge_count), 0)
    onehot = (species_ids == species[None, :]).astype(jnp.float32)
    embedding = lax.optimization_barrier(jnp.sum(species_table[:, :, None] * onehot[None, :, :], axis=1))
    embedded = (scalars.astype(jnp.float32) + embedding).astype(jnp.bfloat16)
    queries = jnp.dot(w_query, embedded, preferred_element_type=jnp.float32)
    key_rows = jnp.dot(w_key, scalar_rev, preferred_element_type=jnp.float32)
    values = jnp.dot(w_value, scalar_rev, preferred_element_type=jnp.float32)
    head_size = channels // HEADS
    scores = lax.optimization_barrier(jnp.sum((queries * key_rows).reshape(HEADS, head_size, edge_count), axis=1)) / math.sqrt(head_size)
    attention = jax.nn.sigmoid(scores)
    attended = (attention[:, None, :] * values.reshape(HEADS, head_size, edge_count)).reshape(channels, edge_count).astype(jnp.bfloat16)
    product = tensors.astype(jnp.float32) * tensor_rev.astype(jnp.float32)
    invariant = jnp.concatenate([product[0], lax.optimization_barrier(jnp.sum(product[1:4], axis=0)), lax.optimization_barrier(jnp.sum(product[4:9], axis=0))], axis=0).astype(jnp.bfloat16)
    middle = (embedded.astype(jnp.float32) + jnp.dot(w_output, attended, preferred_element_type=jnp.float32) + jnp.dot(w_invariant, invariant, preferred_element_type=jnp.float32)).astype(jnp.bfloat16)
    message = jnp.dot(w_message, middle, preferred_element_type=jnp.float32).astype(jnp.bfloat16)
    slot_count = received.shape[1]
    target = jnp.where(reverse >= edge_count, reverse - edge_count, slot_count).astype(jnp.int32)
    returned = jnp.zeros((channels, slot_count), jnp.bfloat16).at[:, target].add(message, mode='drop')
    tensor_gate = jax.nn.sigmoid(jnp.dot(w_gate, middle, preferred_element_type=jnp.float32)).reshape(3, multiplicity, edge_count)
    radial = jnp.dot(w_radial, middle, preferred_element_type=jnp.float32).reshape(3, multiplicity, edge_count)
    mixed_rev = jnp.einsum('oi,cie->coe', w_mixing.astype(jnp.float32), tensor_rev.astype(jnp.float32))
    harmonic = solid_harmonics(vectors)
    new_tensors = (tensors.astype(jnp.float32) + by_degree(tensor_gate) * mixed_rev + by_degree(radial) * harmonic[:, None, :]).astype(jnp.bfloat16)
    return (middle, message, returned, new_tensors)

def finish(middle, message, reverse, send_index, counts, returns, w_expand, w_reverse, w_contract):
    channels, edge_count = middle.shape
    local_part = jnp.take(message, jnp.minimum(reverse, edge_count - 1), axis=1).astype(jnp.float32)
    local_part = jnp.where((reverse < edge_count)[None, :], local_part, jnp.float32(0.0))
    live_slots = (lax.broadcasted_iota(jnp.int32, send_index.shape, 1) < counts[:, None]).reshape(-1)
    arrived = jnp.where(live_slots[None, :], returns.astype(jnp.float32), jnp.float32(0.0))
    incoming = (local_part + jnp.zeros((channels, edge_count), jnp.float32).at[:, send_index.reshape(-1)].add(arrived)).astype(jnp.bfloat16)
    hidden = jax.nn.silu(jnp.dot(w_expand, middle, preferred_element_type=jnp.float32) + jnp.dot(w_reverse, incoming, preferred_element_type=jnp.float32)).astype(jnp.bfloat16)
    return (middle.astype(jnp.float32) + jnp.dot(w_contract, hidden, preferred_element_type=jnp.float32)).astype(jnp.bfloat16)

def reference(scalars, tensors, vectors, species, species_table, reverse, send_index, counts, w_query, w_key, w_value, w_output, w_invariant, w_message, w_gate, w_radial, w_mixing, w_expand, w_reverse, w_contract):
    extent_x, extent_y = (scalars.shape[0], scalars.shape[1])
    domains = extent_x * extent_y

    def flatten(array):
        return array.reshape((domains,) + array.shape[2:])

    def grid(array):
        return array.reshape((extent_x, extent_y) + array.shape[1:])
    block_width = send_index.shape[-1]
    outgoing = grid(lax.map(lambda packed: send_blocks(*packed), (flatten(scalars), flatten(tensors), flatten(send_index), flatten(counts))))
    received = jnp.concatenate([jnp.roll(outgoing[..., position * block_width:(position + 1) * block_width], (step_x, step_y), axis=(0, 1)) for position, (step_x, step_y) in enumerate(DIRECTIONS)], axis=-1)
    weights = (w_query, w_key, w_value, w_output, w_invariant, w_message, w_gate, w_radial, w_mixing)
    middle, message, returned, new_tensors = lax.map(lambda packed: edge_update(*packed, species_table, weights), (flatten(scalars), flatten(tensors), flatten(vectors), flatten(species), flatten(reverse), flatten(received)))
    returned = grid(returned)
    returns = jnp.concatenate([jnp.roll(returned[..., position * block_width:(position + 1) * block_width], (-step_x, -step_y), axis=(0, 1)) for position, (step_x, step_y) in enumerate(DIRECTIONS)], axis=-1)
    result = lax.map(lambda packed: finish(*packed, w_expand, w_reverse, w_contract), (middle, message, flatten(reverse), flatten(send_index), flatten(counts), flatten(returns)))
    return (result.reshape(scalars.shape), new_tensors.reshape(tensors.shape))
```

```python
import functools
import math

import jax
import jax.numpy as jnp
from jax import lax
from jax.experimental import pallas as pl
from jax.experimental.pallas import tpu as pltpu
from jax.sharding import PartitionSpec as P

MESH = pl.DeviceIdType.MESH
HEADS = 8
DIRECTIONS = ((1, 0), (-1, 0), (0, 1), (0, -1), (1, 1), (1, -1), (-1, 1), (-1, -1))
OPPOSITE = (1, 0, 3, 2, 7, 6, 5, 4)
C = 256
MUL = 64
ROWS_T = 9 * MUL
ROWS = C + ROWS_T
FFN = 512
E = 2048
BLOCK = 64
SLOTS = 8 * BLOCK
EXTRA = 16
TILE = 256
PAIR = 2 * BLOCK
GROUPS = SLOTS // PAIR
DEGREE = (0, 1, 1, 1, 2, 2, 2, 2, 2)
BF = jnp.bfloat16
F32 = jnp.float32


def dot(a, b):
    return jnp.dot(a, b, preferred_element_type=F32)


def sigmoid(v):
    return 0.5 * jnp.tanh(0.5 * v) + 0.5


def one_hot(rows, first, ids):
    iota = lax.broadcasted_iota(jnp.int32, (rows, ids.shape[1]), 0)
    return jnp.where(iota == ids - first, 1.0, 0.0).astype(BF)


def slot_of(reverse):
    away = reverse - E
    block = lax.shift_right_logical(away, 6)
    partner = jnp.where(block < 4, jnp.bitwise_xor(block, 1), 11 - block)
    return jnp.where(reverse < E, -1, partner * BLOCK + jnp.bitwise_and(away, BLOCK - 1))


def harmonics(x, y, z):
    r2 = x * x + y * y + z * z
    root = math.sqrt(3.0)
    return (None, x, y, z, root * x * y, root * y * z, 0.5 * (3.0 * z * z - r2), root * x * z, 0.5 * root * (x * x - y * y))


def embed(scalars, table, species):
    n = scalars.shape[1]
    parts = []
    for lane in range(0, n, 128):
        sp = species[:, lane : lane + 128]
        t = [table[j] for j in range(4)]
        low = jnp.where(sp == 0, t[0], t[1])
        high = jnp.where(sp == 2, t[2], t[3])
        parts.append(scalars[:, lane : lane + 128].astype(F32) + jnp.where(sp < 2, low, high))
    return (parts[0] if len(parts) == 1 else jnp.concatenate(parts, axis=1)).astype(BF)


def invariants(tensors, tensors_rev):
    sums = [None, None, None]
    for k in range(9):
        term = tensors(k).astype(F32) * tensors_rev(k).astype(F32)
        d = DEGREE[k]
        sums[d] = term if sums[d] is None else sums[d] + term
    return jnp.concatenate(sums, axis=0).astype(BF)


def middle_of(embedded, scalars_rev, invariant, wq, wkv, wo, wi):
    n = embedded.shape[1]
    head = C // HEADS
    queries = dot(wq[...], embedded)
    kv = dot(wkv[...], scalars_rev)
    scores = jnp.sum((queries * kv[:C]).reshape(HEADS, head, n), axis=1, keepdims=True)
    attention = sigmoid(scores * (1.0 / math.sqrt(head)))
    attended = (attention * kv[C:].reshape(HEADS, head, n)).reshape(C, n).astype(BF)
    return (embedded.astype(F32) + dot(wo[...], attended) + dot(wi[...], invariant)).astype(BF)


def update_tensors(k, tensor, tensor_rev, gate, radial, harmonic, wx):
    d = DEGREE[k]
    rows = slice(d * MUL, (d + 1) * MUL)
    mixed = dot(wx[...], tensor_rev)
    last = radial[rows] if harmonic is None else radial[rows] * harmonic
    return (tensor.astype(F32) + gate[rows] * mixed + last).astype(BF)


def feed_forward(middle, incoming, wer, wc):
    v = dot(wer[...], jnp.concatenate([middle, incoming], axis=0))
    hidden = (v * sigmoid(v)).astype(BF)
    return (middle.astype(F32) + dot(wc[...], hidden)).astype(BF)


def exchange_kernel(
    nx, ny,
    scalars_h, tensors_h, vectors_h, species_h, table_h, reverse_h, send_h,
    wq_h, wk_h, wv_h, wo_h, wi_h, wm_h, wg_h, wr_h, wx_h, we_h, wrev_h, wc_h,
    part_h, last_h,
    x, xe, vec, spc, tab, rev, sidx,
    wq, wkv, wo, wit, wi, wmgr, wx, wer, wc,
    g, p, rev_t, own, send_a, send_b, recv_a, recv_b, send_s, recv_s,
    mid, msg, out, y, tb,
    load_sem, send_sem, recv_sem, store_sem,
):
    gx, gy = lax.axis_index("gx"), lax.axis_index("gy")
    partners = [(lax.rem(gx + dx + nx, nx), lax.rem(gy + dy + ny, ny)) for dx, dy in DIRECTIONS]
    barrier = pltpu.get_barrier_semaphore()
    for partner in partners:
        pl.semaphore_signal(barrier, inc=1, device_id=partner, device_id_type=MESH)

    loads = {}

    def load(name, src, dst):
        copy = pltpu.make_async_copy(src, dst, load_sem.at[len(loads)])
        copy.start()
        loads[name] = copy

    load("send", send_h, sidx)
    load("scalars", scalars_h, x.at[pl.ds(0, C)])
    load("tensors", tensors_h, x.at[pl.ds(C, ROWS_T)])
    load("vectors", vectors_h, vec)
    load("species", species_h, spc)
    load("reverse", reverse_h, rev)
    load("table", table_h, tab)
    load("wq", wq_h, wq)
    load("wk", wk_h, wkv.at[pl.ds(0, C)])
    load("wv", wv_h, wkv.at[pl.ds(C, C)])
    load("wo", wo_h, wo)
    load("wi", wi_h, wit)
    load("wm", wm_h, wmgr.at[pl.ds(0, C)])
    load("wg", wg_h, wmgr.at[pl.ds(C, 3 * MUL)])
    load("wr", wr_h, wmgr.at[pl.ds(C + 3 * MUL, 3 * MUL)])
    load("wx", wx_h, wx)
    load("we", we_h, wer.at[:, pl.ds(0, C)])
    load("wrev", wrev_h, wer.at[:, pl.ds(C, C)])
    load("wc", wc_h, wc)

    loads["send"].wait()
    lane = lax.broadcasted_iota(jnp.int32, (1, PAIR), 1)

    def ids_of(pair):
        a, b = sidx[2 * pair : 2 * pair + 1, :], sidx[2 * pair + 1 : 2 * pair + 2, :]
        return jnp.concatenate([a, b], axis=1)

    def pack(block, pair, dst):
        h = block.shape[0] // 2
        top, bottom = block[:h], block[h:]
        dst[2 * pair] = jnp.where(lane < BLOCK, top, pltpu.roll(bottom, BLOCK, 1)).astype(BF)
        dst[2 * pair + 1] = jnp.where(lane < BLOCK, pltpu.roll(top, BLOCK, 1), bottom).astype(BF)

    copies_a, copies_b, copies_s = [], [], []
    for d in range(8):
        o = OPPOSITE[d]
        for kind, (copies, src, dst) in enumerate(
            (
                (copies_a, send_a.at[d], recv_a.at[o]),
                (copies_b, send_b.at[d], recv_b.at[o]),
                (copies_s, send_s.at[pl.ds(d, 1)], recv_s.at[pl.ds(o, 1)]),
            )
        ):
            copies.append(
                pltpu.make_async_remote_copy(
                    src_ref=src,
                    dst_ref=dst,
                    send_sem=send_sem.at[kind, d],
                    recv_sem=recv_sem.at[kind, o],
                    device_id=partners[d],
                    device_id_type=MESH,
                )
            )

    for half in range(2):
        cols = pl.ds(half * TILE, TILE)
        ids = jnp.concatenate([ids_of(2 * half), ids_of(2 * half + 1)], axis=1)
        g[:, cols] = one_hot(E, 0, ids)
        if half == 0:
            loads["scalars"].wait()
        picked = dot(x[pl.ds(0, C)], g[:, cols])
        own[pl.ds(0, C), cols] = picked.astype(BF)
        for j in range(2):
            pack(picked[:, j * PAIR : (j + 1) * PAIR], 2 * half + j, send_a)
        if half == 0:
            pl.semaphore_wait(barrier, 8)
        for d in range(4 * half, 4 * half + 4):
            copies_a[d].start()
        if half == 0:
            loads["tensors"].wait()
        picked = dot(x[pl.ds(C, ROWS_T)], g[:, cols])
        own[pl.ds(C, ROWS_T), cols] = picked.astype(BF)
        for j in range(2):
            pack(picked[:, j * PAIR : (j + 1) * PAIR], 2 * half + j, send_b)
        for d in range(4 * half, 4 * half + 4):
            copies_b[d].start()

    loads["vectors"].wait()
    loads["species"].wait()
    v = [vec[k] for k in range(3)]
    high = [u.astype(BF).astype(F32) for u in v]
    middle = [(a - b).astype(BF).astype(F32) for a, b in zip(v, high)]
    low = [a - b - c for a, b, c in zip(v, high, middle)]
    species_row = spc[...].astype(F32)
    xe[...] = jnp.concatenate(high + middle + low + [species_row] + [jnp.zeros_like(species_row)] * (EXTRA - 10), axis=0).astype(BF)
    extra = dot(xe[...], g[...])
    own_vec = [extra[k : k + 1] + (extra[3 + k : 4 + k] + extra[6 + k : 7 + k]) for k in range(3)]
    own_species = extra[9:10]
    for pair in range(GROUPS):
        s = own_species[:, pair * PAIR : (pair + 1) * PAIR]
        send_s[2 * pair : 2 * pair + 1] = s
        send_s[2 * pair + 1 : 2 * pair + 2] = pltpu.roll(s, BLOCK, 1)
    for d in range(8):
        copies_s[d].start()

    loads["table"].wait()
    for j in range(4):
        for h in range(2):
            row = tab[j : j + 1, h * 128 : (h + 1) * 128]
            tb[j, pl.ds(h * 128, 128)] = jnp.broadcast_to(row, (128, 128)).T
    for name in ("reverse", "wq", "wk", "wv", "wo", "wi", "wm", "wg", "wr", "wx", "we", "wrev", "wc"):
        loads[name].wait()
    wi[...] = wit[...].astype(F32).T.astype(BF)

    def first_tile(t, carry):
        cols = pl.ds(pl.multiple_of(t * TILE, TILE), TILE)
        ids = rev[:, cols]
        p[:, cols] = one_hot(E, 0, ids)
        rev_t[...] = dot(x[...], p[:, cols]).astype(BF)
        embedded = embed(x[pl.ds(0, C), cols], tb, spc[:, cols])
        invariant = invariants(
            lambda k: x[pl.ds(C + k * MUL, MUL), cols], lambda k: rev_t[pl.ds(C + k * MUL, MUL)]
        )
        m = middle_of(embedded, rev_t[pl.ds(0, C)], invariant, wq, wkv, wo, wi)
        mid[:, cols] = m
        mgr = dot(wmgr[...], m)
        msg[:, cols] = mgr[:C].astype(BF)
        gate = sigmoid(mgr[C : C + 3 * MUL])
        radial = mgr[C + 3 * MUL :]
        harmonic = harmonics(vec[0, :, cols], vec[1, :, cols], vec[2, :, cols])
        local = ids < E
        for k in range(9):
            rows = pl.ds(C + k * MUL, MUL)
            new = update_tensors(k, x[rows, cols], rev_t[rows], gate, radial, harmonic[k], wx)
            out[rows, cols] = jnp.where(local, new.astype(F32), 0.0).astype(BF)
        return carry

    lax.fori_loop(0, E // TILE, first_tile, 0)

    def second_tile(t, carry):
        cols = pl.ds(pl.multiple_of(t * TILE, TILE), TILE)
        incoming = dot(msg[...], p[:, cols]).astype(BF)
        new = feed_forward(mid[:, cols], incoming, wer, wc)
        out[pl.ds(0, C), cols] = jnp.where(rev[:, cols] < E, new.astype(F32), 0.0).astype(BF)
        return carry

    lax.fori_loop(0, E // TILE, second_tile, 0)

    def unpack(a, b):
        a, b = a.astype(F32), b.astype(F32)
        top = jnp.where(lane < BLOCK, a, pltpu.roll(b, BLOCK, 1))
        bottom = jnp.where(lane < BLOCK, pltpu.roll(a, BLOCK, 1), b)
        return jnp.concatenate([top, bottom], axis=0).astype(BF)

    for pair in range(GROUPS):
        cols = pl.ds(pair * PAIR, PAIR)
        for d in (2 * pair, 2 * pair + 1):
            copies_a[OPPOSITE[d]].wait_recv()
            copies_s[OPPOSITE[d]].wait_recv()
        here = own[pl.ds(0, C), cols]
        there = unpack(recv_a[2 * pair], recv_a[2 * pair + 1])
        species_there = jnp.where(
            lane < BLOCK, recv_s[2 * pair : 2 * pair + 1], pltpu.roll(recv_s[2 * pair + 1 : 2 * pair + 2], BLOCK, 1)
        )
        species_both = jnp.concatenate([own_species[:, pair * PAIR : (pair + 1) * PAIR], species_there], axis=1)
        embedded = embed(jnp.concatenate([here, there], axis=1), tb, species_both)
        for d in (2 * pair, 2 * pair + 1):
            copies_b[OPPOSITE[d]].wait_recv()
        rev_t[pl.ds(C, ROWS_T), pl.ds(0, PAIR)] = unpack(recv_b[2 * pair], recv_b[2 * pair + 1])
        invariant = invariants(
            lambda k: own[pl.ds(C + k * MUL, MUL), cols], lambda k: rev_t[pl.ds(C + k * MUL, MUL), pl.ds(0, PAIR)]
        )
        m = middle_of(
            embedded,
            jnp.concatenate([there, here], axis=1),
            jnp.concatenate([invariant, invariant], axis=1),
            wq, wkv, wo, wi,
        )
        mgr = dot(wmgr[...], m)
        gate = sigmoid(mgr[C : C + 3 * MUL, :PAIR])
        radial = mgr[C + 3 * MUL :, :PAIR]
        harmonic = harmonics(*[u[:, pair * PAIR : (pair + 1) * PAIR] for u in own_vec])
        for k in range(9):
            rows = pl.ds(C + k * MUL, MUL)
            y[rows, cols] = update_tensors(
                k, own[rows, cols], rev_t[rows, pl.ds(0, PAIR)], gate, radial, harmonic[k], wx
            )
        y[pl.ds(0, C), cols] = feed_forward(m[:, :PAIR], mgr[:C, PAIR:].astype(BF), wer, wc)
        if pair == GROUPS - 2:
            done = (pair + 1) * PAIR

            def place(t, carry):
                tile = pl.ds(pl.multiple_of(t * TILE, TILE), TILE)
                hot = one_hot(done, 0, slot_of(rev[:, tile]))
                add = dot(y[:, pl.ds(0, done)], hot)
                out[:, tile] = (out[:, tile].astype(F32) + add).astype(BF)
                return carry

            lax.fori_loop(0, E // TILE, place, 0)
            store = pltpu.make_async_copy(out, part_h, store_sem.at[0])
            store.start()
    last = pltpu.make_async_copy(y.at[:, pl.ds((GROUPS - 1) * PAIR, PAIR)], last_h, store_sem.at[1])
    last.start()
    for d in range(8):
        copies_a[d].wait_send()
        copies_b[d].wait_send()
        copies_s[d].wait_send()
    store.wait()
    last.wait()


CHUNKS = (64, 192, 192, 192, 192)


def final_kernel(part_h, last_h, reverse_h, scalars_h, tensors_h, part, last, rev, hot, load_sem, store_sem):
    loads = []

    def load(src, dst):
        copy = pltpu.make_async_copy(src, dst, load_sem.at[len(loads)])
        copy.start()
        loads.append(copy)

    load(reverse_h, rev)
    load(last_h, last)
    starts = [sum(CHUNKS[:i]) for i in range(len(CHUNKS))]
    for start, rows in zip(starts, CHUNKS):
        load(part_h.at[pl.ds(start, rows)], part.at[pl.ds(start, rows)])
    loads[0].wait()
    hot[...] = one_hot(PAIR, (GROUPS - 1) * PAIR, slot_of(rev[...]))
    loads[1].wait()
    stores = []
    for i, (start, rows) in enumerate(zip(starts, CHUNKS)):
        loads[2 + i].wait()
        for t in range(0, E, 512):
            add = dot(last[pl.ds(start, rows)], hot[:, pl.ds(t, 512)])
            part[pl.ds(start, rows), pl.ds(t, 512)] = (part[pl.ds(start, rows), pl.ds(t, 512)].astype(F32) + add).astype(BF)
        dst = scalars_h.at[pl.ds(start, rows)] if start < C else tensors_h.at[pl.ds(start - C, rows)]
        copy = pltpu.make_async_copy(part.at[pl.ds(start, rows)], dst, store_sem.at[i])
        copy.start()
        stores.append(copy)
    for copy in stores:
        copy.wait()


def per_device(
    nx, ny,
    scalars, tensors, vectors, species, species_table, reverse, send_index, counts,
    w_query, w_key, w_value, w_output, w_invariant, w_message, w_gate, w_radial, w_mixing, w_expand, w_reverse, w_contract,
):
    reverse_row = reverse.reshape(1, E)
    hbm = pl.BlockSpec(memory_space=pltpu.HBM)
    part, last = pl.pallas_call(
        functools.partial(exchange_kernel, nx, ny),
        out_shape=(jax.ShapeDtypeStruct((ROWS, E), BF), jax.ShapeDtypeStruct((ROWS, PAIR), BF)),
        in_specs=[hbm] * 19,
        out_specs=(hbm, hbm),
        scratch_shapes=[
            pltpu.VMEM((ROWS, E), BF),
            pltpu.VMEM((EXTRA, E), BF),
            pltpu.VMEM((3, 1, E), F32),
            pltpu.VMEM((1, E), jnp.int32),
            pltpu.VMEM((4, C), F32),
            pltpu.VMEM((1, E), jnp.int32),
            pltpu.VMEM((8, BLOCK), jnp.int32),
            pltpu.VMEM((C, C), BF),
            pltpu.VMEM((2 * C, C), BF),
            pltpu.VMEM((C, C), BF),
            pltpu.VMEM((3 * MUL, C), BF),
            pltpu.VMEM((C, 3 * MUL), BF),
            pltpu.VMEM((C + 6 * MUL, C), BF),
            pltpu.VMEM((MUL, MUL), BF),
            pltpu.VMEM((FFN, 2 * C), BF),
            pltpu.VMEM((C, FFN), BF),
            pltpu.VMEM((E, SLOTS), BF),
            pltpu.VMEM((E, E), BF),
            pltpu.VMEM((ROWS, TILE), BF),
            pltpu.VMEM((ROWS, SLOTS), BF),
            pltpu.VMEM((8, C // 2, 128), BF),
            pltpu.VMEM((8, ROWS_T // 2, 128), BF),
            pltpu.VMEM((8, C // 2, 128), BF),
            pltpu.VMEM((8, ROWS_T // 2, 128), BF),
            pltpu.VMEM((8, 128), F32),
            pltpu.VMEM((8, 128), F32),
            pltpu.VMEM((C, E), BF),
            pltpu.VMEM((C, E), BF),
            pltpu.VMEM((ROWS, E), BF),
            pltpu.VMEM((ROWS, SLOTS), BF),
            pltpu.VMEM((4, C, 128), F32),
            pltpu.SemaphoreType.DMA((19,)),
            pltpu.SemaphoreType.DMA((3, 8)),
            pltpu.SemaphoreType.DMA((3, 8)),
            pltpu.SemaphoreType.DMA((2,)),
        ],
        compiler_params=pltpu.CompilerParams(collective_id=0, has_side_effects=True, vmem_limit_bytes=int(60 * 2**20)),
        cost_estimate=pl.CostEstimate(flops=16 * 10**9, bytes_accessed=9 * 2**20, transcendentals=3 * 10**6),
        name="exchange",
    )(
        scalars.reshape(C, E), tensors.reshape(ROWS_T, E), vectors.reshape(3, 1, E), species.reshape(1, E),
        species_table.T, reverse_row, send_index.reshape(8, BLOCK),
        w_query, w_key, w_value, w_output, w_invariant.T, w_message, w_gate, w_radial, w_mixing,
        w_expand, w_reverse, w_contract,
    )
    new_scalars, new_tensors = pl.pallas_call(
        final_kernel,
        out_shape=(jax.ShapeDtypeStruct((C, E), BF), jax.ShapeDtypeStruct((ROWS_T, E), BF)),
        in_specs=[hbm] * 3,
        out_specs=(hbm, hbm),
        scratch_shapes=[
            pltpu.VMEM((ROWS, E), BF),
            pltpu.VMEM((ROWS, PAIR), BF),
            pltpu.VMEM((1, E), jnp.int32),
            pltpu.VMEM((PAIR, E), BF),
            pltpu.SemaphoreType.DMA((2 + len(CHUNKS),)),
            pltpu.SemaphoreType.DMA((len(CHUNKS),)),
        ],
        compiler_params=pltpu.CompilerParams(vmem_limit_bytes=int(56 * 2**20)),
        cost_estimate=pl.CostEstimate(flops=10**9, bytes_accessed=7 * 2**20, transcendentals=0),
        name="combine",
    )(part, last, reverse_row)
    return new_scalars.reshape(1, 1, C, E), new_tensors.reshape(1, 1, 9, MUL, E)


def solution(mesh):
    split = P("gx", "gy")
    return jax.shard_map(
        functools.partial(per_device, mesh.shape["gx"], mesh.shape["gy"]),
        mesh=mesh,
        in_specs=(split,) * 4 + (P(),) + (split,) * 3 + (P(),) * 12,
        out_specs=(split, split),
        check_vma=False,
    )
```

```python
import functools
import math

import jax
import jax.numpy as jnp
from jax import lax
from jax.experimental import pallas as pl
from jax.experimental.pallas import tpu as pltpu
from jax.sharding import PartitionSpec as P

MESH = pl.DeviceIdType.MESH
HEADS = 8
DIRECTIONS = ((1, 0), (-1, 0), (0, 1), (0, -1), (1, 1), (1, -1), (-1, 1), (-1, -1))
OPPOSITE = (1, 0, 3, 2, 7, 6, 5, 4)
C = 256
MUL = 64
ROWS_T = 9 * MUL
ROWS = C + ROWS_T
FFN = 512
E = 2048
BLOCK = 64
SLOTS = 8 * BLOCK
EXTRA = 16
TILE = 256
PAIR = 2 * BLOCK
GROUPS = SLOTS // PAIR
ARRIVAL = (0, 1, 3, 2)
EARLY = 2 * PAIR
DEGREE = (0, 1, 1, 1, 2, 2, 2, 2, 2)
BF = jnp.bfloat16
F32 = jnp.float32


def dot(a, b):
    return jnp.dot(a, b, preferred_element_type=F32)


def sigmoid(v):
    return 0.5 * jnp.tanh(0.5 * v) + 0.5


def one_hot(rows, first, ids):
    iota = lax.broadcasted_iota(jnp.int32, (rows, ids.shape[1]), 0)
    return jnp.where(iota == ids - first, 1.0, 0.0).astype(BF)


def slot_of(reverse):
    away = reverse - E
    block = lax.shift_right_logical(away, 6)
    partner = jnp.where(block < 4, jnp.bitwise_xor(block, 1), 11 - block)
    return jnp.where(reverse < E, -1, partner * BLOCK + jnp.bitwise_and(away, BLOCK - 1))


def harmonics(x, y, z):
    r2 = x * x + y * y + z * z
    root = math.sqrt(3.0)
    return (None, x, y, z, root * x * y, root * y * z, 0.5 * (3.0 * z * z - r2), root * x * z, 0.5 * root * (x * x - y * y))


def embed(scalars, table, species):
    n = scalars.shape[1]
    parts = []
    for lane in range(0, n, 128):
        sp = species[:, lane : lane + 128]
        t = [table[j] for j in range(4)]
        low = jnp.where(sp == 0, t[0], t[1])
        high = jnp.where(sp == 2, t[2], t[3])
        parts.append(scalars[:, lane : lane + 128].astype(F32) + jnp.where(sp < 2, low, high))
    return (parts[0] if len(parts) == 1 else jnp.concatenate(parts, axis=1)).astype(BF)


def invariants(tensors, tensors_rev):
    sums = [None, None, None]
    for k in range(9):
        term = tensors(k).astype(F32) * tensors_rev(k).astype(F32)
        d = DEGREE[k]
        sums[d] = term if sums[d] is None else sums[d] + term
    return jnp.concatenate(sums, axis=0).astype(BF)


def edge_update(tensors, tensors_rev, embedded, scalars_turned, harmonic, wq, wkv, wo, wi, wm, wgr, wx, wer, wc, store):
    n = embedded.shape[1] // 2
    head = C // HEADS
    queries = dot(wq[...], embedded)
    kv = dot(wkv[...], scalars_turned)
    scores = jnp.sum((queries * kv[:C]).reshape(HEADS, head, 2 * n), axis=1, keepdims=True)
    attention = sigmoid(scores * (1.0 / math.sqrt(head)))
    attended = (attention * kv[C:].reshape(HEADS, head, 2 * n)).reshape(C, 2 * n).astype(BF)
    shared = dot(wi[...], invariants(tensors, tensors_rev))
    middles = (embedded.astype(F32) + dot(wo[...], attended) + jnp.concatenate([shared, shared], axis=1)).astype(BF)
    middle = middles[:, :n]
    incoming = dot(wm[...], middles[:, n:]).astype(BF)
    gr = dot(wgr[...], middle)
    for k in range(9):
        d = DEGREE[k]
        mixed = dot(wx[...], tensors_rev(k))
        gate = sigmoid(gr[d * MUL : (d + 1) * MUL])
        radial = gr[(3 + d) * MUL : (4 + d) * MUL]
        last = radial if harmonic[k] is None else radial * harmonic[k]
        store(k, (tensors(k).astype(F32) + gate * mixed + last).astype(BF))
    v = dot(wer[...], jnp.concatenate([middle, incoming], axis=0))
    hidden = (v * sigmoid(v)).astype(BF)
    store(-1, (middle.astype(F32) + dot(wc[...], hidden)).astype(BF))


def exchange_kernel(
    nx, ny,
    scalars_h, tensors_h, vectors_h, species_h, table_h, reverse_h, send_h,
    wq_h, wk_h, wv_h, wo_h, wi_h, wm_h, wg_h, wr_h, wx_h, we_h, wrev_h, wc_h,
    out, y_late,
    x, vec, spc, tab, rev, sidx,
    wq, wkv, wo, wit, wi, wm, wgr, wx, wer, wc,
    g, p0, p1, rev0, rev1, own, send_a, send_b, recv_a, recv_b, send_s, recv_s,
    y, tb,
    load_sem, send_sem, recv_sem,
):
    gx, gy = lax.axis_index("gx"), lax.axis_index("gy")
    partners = [(lax.rem(gx + dx + nx, nx), lax.rem(gy + dy + ny, ny)) for dx, dy in DIRECTIONS]
    barrier = pltpu.get_barrier_semaphore()
    for partner in partners:
        pl.semaphore_signal(barrier, inc=1, device_id=partner, device_id_type=MESH)

    loads = {}

    def load(name, src, dst):
        copy = pltpu.make_async_copy(src, dst, load_sem.at[len(loads)])
        copy.start()
        loads[name] = copy

    load("send", send_h, sidx)
    load("scalars", scalars_h, x.at[pl.ds(0, C)])
    load("tensors", tensors_h, x.at[pl.ds(C, ROWS_T)])
    load("vectors", vectors_h, vec)
    load("species", species_h, spc)

    loads["send"].wait()
    lane = lax.broadcasted_iota(jnp.int32, (1, PAIR), 1)

    def ids_of(pair):
        a, b = sidx[2 * pair : 2 * pair + 1, :], sidx[2 * pair + 1 : 2 * pair + 2, :]
        return jnp.concatenate([a, b], axis=1)

    def pack(block, pair, dst):
        h = block.shape[0] // 2
        top, bottom = block[:h], block[h:]
        dst[2 * pair] = jnp.where(lane < BLOCK, top, pltpu.roll(bottom, BLOCK, 1)).astype(BF)
        dst[2 * pair + 1] = jnp.where(lane < BLOCK, pltpu.roll(top, BLOCK, 1), bottom).astype(BF)

    copies_a, copies_b, copies_s = [], [], []
    for d in range(8):
        o = OPPOSITE[d]
        for kind, (copies, src, dst) in enumerate(
            (
                (copies_a, send_a.at[d], recv_a.at[o]),
                (copies_b, send_b.at[d], recv_b.at[o]),
                (copies_s, send_s.at[pl.ds(d, 1)], recv_s.at[pl.ds(o, 1)]),
            )
        ):
            copies.append(
                pltpu.make_async_remote_copy(
                    src_ref=src,
                    dst_ref=dst,
                    send_sem=send_sem.at[kind, d],
                    recv_sem=recv_sem.at[kind, o],
                    device_id=partners[d],
                    device_id_type=MESH,
                )
            )

    for half in range(2):
        cols = pl.ds(half * TILE, TILE)
        ids = jnp.concatenate([ids_of(2 * half), ids_of(2 * half + 1)], axis=1)
        g[:, cols] = one_hot(E, 0, ids)
        if half == 0:
            loads["scalars"].wait()
        picked = dot(x[pl.ds(0, C)], g[:, cols])
        own[pl.ds(0, C), cols] = picked.astype(BF)
        for j in range(2):
            pack(picked[:, j * PAIR : (j + 1) * PAIR], 2 * half + j, send_a)
        if half == 0:
            pl.semaphore_wait(barrier, 8)
        for d in range(4 * half, 4 * half + 4):
            copies_a[d].start()
        if half == 0:
            load("reverse", reverse_h, rev)
            load("table", table_h, tab)
            load("wq", wq_h, wq)
            load("wk", wk_h, wkv.at[pl.ds(0, C)])
            load("wv", wv_h, wkv.at[pl.ds(C, C)])
            load("wo", wo_h, wo)
            load("wi", wi_h, wit)
            load("wm", wm_h, wm)
            load("wg", wg_h, wgr.at[pl.ds(0, 3 * MUL)])
            load("wr", wr_h, wgr.at[pl.ds(3 * MUL, 3 * MUL)])
            load("wx", wx_h, wx)
            load("we", we_h, wer.at[:, pl.ds(0, C)])
            load("wrev", wrev_h, wer.at[:, pl.ds(C, C)])
            load("wc", wc_h, wc)
            loads["tensors"].wait()
        picked = dot(x[pl.ds(C, ROWS_T)], g[:, cols])
        own[pl.ds(C, ROWS_T), cols] = picked.astype(BF)
        for j in range(2):
            pack(picked[:, j * PAIR : (j + 1) * PAIR], 2 * half + j, send_b)
        for d in range(4 * half, 4 * half + 4):
            copies_b[d].start()

    loads["vectors"].wait()
    loads["species"].wait()
    v = [vec[k] for k in range(3)]
    high = [u.astype(BF).astype(F32) for u in v]
    middle = [(a - b).astype(BF).astype(F32) for a, b in zip(v, high)]
    low = [a - b - c for a, b, c in zip(v, high, middle)]
    species_row = spc[...].astype(F32)
    x[pl.ds(ROWS, EXTRA)] = jnp.concatenate(high + middle + low + [species_row] + [jnp.zeros_like(species_row)] * (EXTRA - 10), axis=0).astype(BF)
    extra = dot(x[pl.ds(ROWS, EXTRA)], g[...])
    own_vec = [extra[k : k + 1] + (extra[3 + k : 4 + k] + extra[6 + k : 7 + k]) for k in range(3)]
    own_species = extra[9:10]
    for pair in range(GROUPS):
        s = own_species[:, pair * PAIR : (pair + 1) * PAIR]
        send_s[2 * pair : 2 * pair + 1] = s
        send_s[2 * pair + 1 : 2 * pair + 2] = pltpu.roll(s, BLOCK, 1)
    for d in range(8):
        copies_s[d].start()

    loads["table"].wait()
    for j in range(4):
        for h in range(2):
            row = tab[j : j + 1, h * 128 : (h + 1) * 128]
            tb[j, pl.ds(h * 128, 128)] = jnp.broadcast_to(row, (128, 128)).T
    for name in ("reverse", "wq", "wk", "wv", "wo", "wi", "wm", "wg", "wr", "wx", "we", "wrev", "wc"):
        loads[name].wait()
    wi[...] = wit[...].astype(F32).T.astype(BF)

    weights = (wq, wkv, wo, wi, wm, wgr, wx, wer, wc)

    def columns(t):
        return pl.ds(t * TILE if isinstance(t, int) else pl.multiple_of(t * TILE, TILE), TILE)

    def gather(t, p, turned):
        p[...] = one_hot(E, 0, rev[:, columns(t)])
        turned[...] = dot(x[...], p[...]).astype(BF)

    def work(t, turned):
        cols = columns(t)
        here, there = x[pl.ds(0, C), cols], turned[pl.ds(0, C)]
        species_there = turned[pl.ds(ROWS, EXTRA)].astype(F32)[9:10]
        embedded = jnp.concatenate([embed(here, tb, spc[:, cols]), embed(there, tb, species_there)], axis=1)

        def store(k, new):
            out[pl.ds(C + k * MUL, MUL) if k >= 0 else pl.ds(0, C), cols] = new

        edge_update(
            lambda k: x[pl.ds(C + k * MUL, MUL), cols],
            lambda k: turned[pl.ds(C + k * MUL, MUL)],
            embedded,
            jnp.concatenate([there, here], axis=1),
            harmonics(vec[0, :, cols], vec[1, :, cols], vec[2, :, cols]),
            *weights,
            store,
        )

    def two_tiles(u, carry):
        gather(2 * u + 1, p1, rev1)
        work(2 * u, rev0)
        gather(2 * u + 2, p0, rev0)
        work(2 * u + 1, rev1)
        return carry

    tiles = E // TILE
    gather(0, p0, rev0)
    lax.fori_loop(0, tiles // 2 - 1, two_tiles, 0)
    gather(tiles - 1, p1, rev1)
    work(tiles - 2, rev0)
    work(tiles - 1, rev1)

    def unpack(a, b):
        a, b = a.astype(F32), b.astype(F32)
        top = jnp.where(lane < BLOCK, a, pltpu.roll(b, BLOCK, 1))
        bottom = jnp.where(lane < BLOCK, pltpu.roll(a, BLOCK, 1), b)
        return jnp.concatenate([top, bottom], axis=0).astype(BF)

    for pair in ARRIVAL:
        cols = pl.ds(pair * PAIR, PAIR)
        for d in (2 * pair, 2 * pair + 1):
            copies_a[OPPOSITE[d]].wait_recv()
            copies_s[OPPOSITE[d]].wait_recv()
        here = own[pl.ds(0, C), cols]
        there = unpack(recv_a[2 * pair], recv_a[2 * pair + 1])
        species_there = jnp.where(
            lane < BLOCK, recv_s[2 * pair : 2 * pair + 1], pltpu.roll(recv_s[2 * pair + 1 : 2 * pair + 2], BLOCK, 1)
        )
        species_both = jnp.concatenate([own_species[:, pair * PAIR : (pair + 1) * PAIR], species_there], axis=1)
        embedded = embed(jnp.concatenate([here, there], axis=1), tb, species_both)
        for d in (2 * pair, 2 * pair + 1):
            copies_b[OPPOSITE[d]].wait_recv()
        rev0[pl.ds(C, ROWS_T), pl.ds(0, PAIR)] = unpack(recv_b[2 * pair], recv_b[2 * pair + 1])

        def store(k, new):
            rows = pl.ds(C + k * MUL, MUL) if k >= 0 else pl.ds(0, C)
            if pair < 2:
                y[rows, cols] = new
            else:
                y_late[rows, pl.ds((pair - 2) * PAIR, PAIR)] = new

        edge_update(
            lambda k: own[pl.ds(C + k * MUL, MUL), cols],
            lambda k: rev0[pl.ds(C + k * MUL, MUL), pl.ds(0, PAIR)],
            embedded,
            jnp.concatenate([there, here], axis=1),
            harmonics(*[u[:, pair * PAIR : (pair + 1) * PAIR] for u in own_vec]),
            *weights,
            store,
        )
        if pair == 1:

            def place(t, carry):
                tile = columns(t)
                slot = slot_of(rev[:, tile])
                moved = dot(y[...], one_hot(EARLY, 0, slot)).astype(BF)
                out[:, tile] = jnp.where((slot >= 0) & (slot < EARLY), moved, out[:, tile])
                return carry

            lax.fori_loop(0, E // TILE, place, 0)
    for d in range(8):
        copies_a[d].wait_send()
        copies_b[d].wait_send()
        copies_s[d].wait_send()


CHUNKS = (192, 64, 192, 192, 192)


def final_kernel(part, last, reverse_h, scalars_h, tensors_h, done, rev, hot, load_sem, store_sem):
    load = pltpu.make_async_copy(reverse_h, rev, load_sem)
    load.start()
    load.wait()
    slot = slot_of(rev[...])
    hot[...] = one_hot(SLOTS - EARLY, EARLY, slot)
    stores = []
    start = 0
    for i, rows in enumerate(CHUNKS):
        for t in range(0, E, 512):
            moved = dot(last[pl.ds(start, rows)], hot[:, pl.ds(t, 512)]).astype(BF)
            block = (pl.ds(start, rows), pl.ds(t, 512))
            done[block] = jnp.where(slot[:, t : t + 512] >= EARLY, moved, part[block])
        dst = scalars_h.at[pl.ds(start, rows)] if start < C else tensors_h.at[pl.ds(start - C, rows)]
        copy = pltpu.make_async_copy(done.at[pl.ds(start, rows)], dst, store_sem.at[i])
        copy.start()
        stores.append(copy)
        start += rows
    for copy in stores:
        copy.wait()


def per_device(
    nx, ny,
    scalars, tensors, vectors, species, species_table, reverse, send_index, counts,
    w_query, w_key, w_value, w_output, w_invariant, w_message, w_gate, w_radial, w_mixing, w_expand, w_reverse, w_contract,
):
    reverse_row = reverse.reshape(1, E)
    hbm = pl.BlockSpec(memory_space=pltpu.HBM)
    vmem = pl.BlockSpec(memory_space=pltpu.VMEM)
    part, last = pl.pallas_call(
        functools.partial(exchange_kernel, nx, ny),
        out_shape=(pltpu.VMEM((ROWS, E), BF), pltpu.VMEM((ROWS, SLOTS - EARLY), BF)),
        in_specs=[hbm] * 19,
        out_specs=(vmem, vmem),
        scratch_shapes=[
            pltpu.VMEM((ROWS + EXTRA, E), BF),
            pltpu.VMEM((3, 1, E), F32),
            pltpu.VMEM((1, E), jnp.int32),
            pltpu.VMEM((4, C), F32),
            pltpu.VMEM((1, E), jnp.int32),
            pltpu.VMEM((8, BLOCK), jnp.int32),
            pltpu.VMEM((C, C), BF),
            pltpu.VMEM((2 * C, C), BF),
            pltpu.VMEM((C, C), BF),
            pltpu.VMEM((3 * MUL, C), BF),
            pltpu.VMEM((C, 3 * MUL), BF),
            pltpu.VMEM((C, C), BF),
            pltpu.VMEM((6 * MUL, C), BF),
            pltpu.VMEM((MUL, MUL), BF),
            pltpu.VMEM((FFN, 2 * C), BF),
            pltpu.VMEM((C, FFN), BF),
            pltpu.VMEM((E, SLOTS), BF),
            pltpu.VMEM((E, TILE), BF),
            pltpu.VMEM((E, TILE), BF),
            pltpu.VMEM((ROWS + EXTRA, TILE), BF),
            pltpu.VMEM((ROWS + EXTRA, TILE), BF),
            pltpu.VMEM((ROWS, SLOTS), BF),
            pltpu.VMEM((8, C // 2, 128), BF),
            pltpu.VMEM((8, ROWS_T // 2, 128), BF),
            pltpu.VMEM((8, C // 2, 128), BF),
            pltpu.VMEM((8, ROWS_T // 2, 128), BF),
            pltpu.VMEM((8, 128), F32),
            pltpu.VMEM((8, 128), F32),
            pltpu.VMEM((ROWS, EARLY), BF),
            pltpu.VMEM((4, C, 128), F32),
            pltpu.SemaphoreType.DMA((19,)),
            pltpu.SemaphoreType.DMA((3, 8)),
            pltpu.SemaphoreType.DMA((3, 8)),
        ],
        compiler_params=pltpu.CompilerParams(collective_id=0, has_side_effects=True, vmem_limit_bytes=int(60 * 2**20)),
        cost_estimate=pl.CostEstimate(flops=16 * 10**9, bytes_accessed=9 * 2**20, transcendentals=3 * 10**6),
        name="exchange",
    )(
        scalars.reshape(C, E), tensors.reshape(ROWS_T, E), vectors.reshape(3, 1, E), species.reshape(1, E),
        species_table.T, reverse_row, send_index.reshape(8, BLOCK),
        w_query, w_key, w_value, w_output, w_invariant.T, w_message, w_gate, w_radial, w_mixing,
        w_expand, w_reverse, w_contract,
    )
    new_scalars, new_tensors = pl.pallas_call(
        final_kernel,
        out_shape=(jax.ShapeDtypeStruct((C, E), BF), jax.ShapeDtypeStruct((ROWS_T, E), BF)),
        in_specs=[vmem, vmem, hbm],
        out_specs=(hbm, hbm),
        scratch_shapes=[
            pltpu.VMEM((ROWS, E), BF),
            pltpu.VMEM((1, E), jnp.int32),
            pltpu.VMEM((SLOTS - EARLY, E), BF),
            pltpu.SemaphoreType.DMA,
            pltpu.SemaphoreType.DMA((len(CHUNKS),)),
        ],
        compiler_params=pltpu.CompilerParams(vmem_limit_bytes=24 * 2**20),
        cost_estimate=pl.CostEstimate(flops=10**9, bytes_accessed=7 * 2**20, transcendentals=0),
        name="combine",
    )(part, last, reverse_row)
    return new_scalars.reshape(1, 1, C, E), new_tensors.reshape(1, 1, 9, MUL, E)


def solution(mesh):
    split = P("gx", "gy")
    return jax.shard_map(
        functools.partial(per_device, mesh.shape["gx"], mesh.shape["gy"]),
        mesh=mesh,
        in_specs=(split,) * 4 + (P(),) + (split,) * 3 + (P(),) * 12,
        out_specs=(split, split),
        check_vma=False,
    )
```

```python
import functools
import math

import jax
import jax.numpy as jnp
from jax import lax
from jax.experimental import pallas as pl
from jax.experimental.pallas import tpu as pltpu
from jax.sharding import PartitionSpec as P

MESH = pl.DeviceIdType.MESH
HEADS = 8
DIRECTIONS = ((1, 0), (-1, 0), (0, 1), (0, -1), (1, 1), (1, -1), (-1, 1), (-1, -1))
OPPOSITE = (1, 0, 3, 2, 7, 6, 5, 4)
C = 256
MUL = 64
ROWS_T = 9 * MUL
ROWS = C + ROWS_T
FFN = 512
E = 2048
BLOCK = 64
SLOTS = 8 * BLOCK
EXTRA = 16
TILE = 256
PAIR = 2 * BLOCK
GROUPS = SLOTS // PAIR
ARRIVAL = (0, 1, 3, 2)
EARLY = 0
DEGREE = (0, 1, 1, 1, 2, 2, 2, 2, 2)
BF = jnp.bfloat16
F32 = jnp.float32


def dot(a, b):
    return jnp.dot(a, b, preferred_element_type=F32)


def sigmoid(v):
    return 0.5 * jnp.tanh(0.5 * v) + 0.5


def one_hot(rows, first, ids):
    iota = lax.broadcasted_iota(jnp.int32, (rows, ids.shape[1]), 0)
    return jnp.where(iota == ids - first, 1.0, 0.0).astype(BF)


def slot_of(reverse):
    away = reverse - E
    block = lax.shift_right_logical(away, 6)
    partner = jnp.where(block < 4, jnp.bitwise_xor(block, 1), 11 - block)
    return jnp.where(reverse < E, -1, partner * BLOCK + jnp.bitwise_and(away, BLOCK - 1))


def harmonics(x, y, z):
    r2 = x * x + y * y + z * z
    root = math.sqrt(3.0)
    return (None, x, y, z, root * x * y, root * y * z, 0.5 * (3.0 * z * z - r2), root * x * z, 0.5 * root * (x * x - y * y))


def embed(scalars, table, species):
    n = scalars.shape[1]
    parts = []
    for lane in range(0, n, 128):
        sp = species[:, lane : lane + 128]
        t = [table[j] for j in range(4)]
        low = jnp.where(sp == 0, t[0], t[1])
        high = jnp.where(sp == 2, t[2], t[3])
        parts.append(scalars[:, lane : lane + 128].astype(F32) + jnp.where(sp < 2, low, high))
    return (parts[0] if len(parts) == 1 else jnp.concatenate(parts, axis=1)).astype(BF)


def invariants(tensors, tensors_rev):
    sums = [None, None, None]
    for k in range(9):
        term = tensors(k).astype(F32) * tensors_rev(k).astype(F32)
        d = DEGREE[k]
        sums[d] = term if sums[d] is None else sums[d] + term
    return jnp.concatenate(sums, axis=0).astype(BF)


def edge_update(tensors, tensors_rev, embedded, scalars_turned, harmonic, wq, wkv, wo, wi, wm, wgr, wx, wer, wc, store):
    n = embedded.shape[1] // 2
    head = C // HEADS
    queries = dot(wq[...], embedded)
    kv = dot(wkv[...], scalars_turned)
    scores = jnp.sum((queries * kv[:C]).reshape(HEADS, head, 2 * n), axis=1, keepdims=True)
    attention = sigmoid(scores * (1.0 / math.sqrt(head)))
    attended = (attention * kv[C:].reshape(HEADS, head, 2 * n)).reshape(C, 2 * n).astype(BF)
    shared = dot(wi[...], invariants(tensors, tensors_rev))
    middles = (embedded.astype(F32) + dot(wo[...], attended) + jnp.concatenate([shared, shared], axis=1)).astype(BF)
    middle = middles[:, :n]
    incoming = dot(wm[...], middles[:, n:]).astype(BF)
    gr = dot(wgr[...], middle)
    for k in range(9):
        d = DEGREE[k]
        mixed = dot(wx[...], tensors_rev(k))
        gate = sigmoid(gr[d * MUL : (d + 1) * MUL])
        radial = gr[(3 + d) * MUL : (4 + d) * MUL]
        last = radial if harmonic[k] is None else radial * harmonic[k]
        store(k, (tensors(k).astype(F32) + gate * mixed + last).astype(BF))
    v = dot(wer[...], jnp.concatenate([middle, incoming], axis=0))
    hidden = (v * sigmoid(v)).astype(BF)
    store(-1, (middle.astype(F32) + dot(wc[...], hidden)).astype(BF))


def exchange_kernel(
    nx, ny,
    scalars_h, tensors_h, vectors_h, species_h, table_h, reverse_h, send_h,
    wq_h, wk_h, wv_h, wo_h, wi_h, wm_h, wg_h, wr_h, wx_h, we_h, wrev_h, wc_h,
    out, y_late,
    x, vec, spc, tab, rev, sidx,
    wq, wkv, wo, wit, wi, wm, wgr, wx, wer, wc,
    g, p0, p1, rev0, rev1, own, send_a, send_b, recv_a, recv_b, send_s, recv_s,
    tb,
    load_sem, send_sem, recv_sem,
):
    gx, gy = lax.axis_index("gx"), lax.axis_index("gy")
    partners = [(lax.rem(gx + dx + nx, nx), lax.rem(gy + dy + ny, ny)) for dx, dy in DIRECTIONS]
    barrier = pltpu.get_barrier_semaphore()
    for partner in partners:
        pl.semaphore_signal(barrier, inc=1, device_id=partner, device_id_type=MESH)

    loads = {}

    def load(name, src, dst):
        copy = pltpu.make_async_copy(src, dst, load_sem.at[len(loads)])
        copy.start()
        loads[name] = copy

    load("send", send_h, sidx)
    load("scalars", scalars_h, x.at[pl.ds(0, C)])
    load("tensors", tensors_h, x.at[pl.ds(C, ROWS_T)])
    load("vectors", vectors_h, vec)
    load("species", species_h, spc)

    loads["send"].wait()
    lane = lax.broadcasted_iota(jnp.int32, (1, PAIR), 1)

    def ids_of(pair):
        a, b = sidx[2 * pair : 2 * pair + 1, :], sidx[2 * pair + 1 : 2 * pair + 2, :]
        return jnp.concatenate([a, b], axis=1)

    def pack(block, pair, dst):
        h = block.shape[0] // 2
        top, bottom = block[:h], block[h:]
        dst[2 * pair] = jnp.where(lane < BLOCK, top, pltpu.roll(bottom, BLOCK, 1)).astype(BF)
        dst[2 * pair + 1] = jnp.where(lane < BLOCK, pltpu.roll(top, BLOCK, 1), bottom).astype(BF)

    copies_a, copies_b, copies_s = [], [], []
    for d in range(8):
        o = OPPOSITE[d]
        for kind, (copies, src, dst) in enumerate(
            (
                (copies_a, send_a.at[d], recv_a.at[o]),
                (copies_b, send_b.at[d], recv_b.at[o]),
                (copies_s, send_s.at[pl.ds(d, 1)], recv_s.at[pl.ds(o, 1)]),
            )
        ):
            copies.append(
                pltpu.make_async_remote_copy(
                    src_ref=src,
                    dst_ref=dst,
                    send_sem=send_sem.at[kind, d],
                    recv_sem=recv_sem.at[kind, o],
                    device_id=partners[d],
                    device_id_type=MESH,
                )
            )

    for half in range(2):
        cols = pl.ds(half * TILE, TILE)
        ids = jnp.concatenate([ids_of(2 * half), ids_of(2 * half + 1)], axis=1)
        g[:, cols] = one_hot(E, 0, ids)
        if half == 0:
            loads["scalars"].wait()
        picked = dot(x[pl.ds(0, C)], g[:, cols])
        own[pl.ds(0, C), cols] = picked.astype(BF)
        for j in range(2):
            pack(picked[:, j * PAIR : (j + 1) * PAIR], 2 * half + j, send_a)
        if half == 0:
            pl.semaphore_wait(barrier, 8)
        for d in range(4 * half, 4 * half + 4):
            copies_a[d].start()
        if half == 0:
            load("reverse", reverse_h, rev)
            load("table", table_h, tab)
            load("wq", wq_h, wq)
            load("wk", wk_h, wkv.at[pl.ds(0, C)])
            load("wv", wv_h, wkv.at[pl.ds(C, C)])
            load("wo", wo_h, wo)
            load("wi", wi_h, wit)
            load("wm", wm_h, wm)
            load("wg", wg_h, wgr.at[pl.ds(0, 3 * MUL)])
            load("wr", wr_h, wgr.at[pl.ds(3 * MUL, 3 * MUL)])
            load("wx", wx_h, wx)
            load("we", we_h, wer.at[:, pl.ds(0, C)])
            load("wrev", wrev_h, wer.at[:, pl.ds(C, C)])
            load("wc", wc_h, wc)
            loads["tensors"].wait()
        picked = dot(x[pl.ds(C, ROWS_T)], g[:, cols])
        own[pl.ds(C, ROWS_T), cols] = picked.astype(BF)
        for j in range(2):
            pack(picked[:, j * PAIR : (j + 1) * PAIR], 2 * half + j, send_b)
        for d in range(4 * half, 4 * half + 4):
            copies_b[d].start()

    loads["vectors"].wait()
    loads["species"].wait()
    v = [vec[k] for k in range(3)]
    high = [u.astype(BF).astype(F32) for u in v]
    middle = [(a - b).astype(BF).astype(F32) for a, b in zip(v, high)]
    low = [a - b - c for a, b, c in zip(v, high, middle)]
    species_row = spc[...].astype(F32)
    x[pl.ds(ROWS, EXTRA)] = jnp.concatenate(high + middle + low + [species_row] + [jnp.zeros_like(species_row)] * (EXTRA - 10), axis=0).astype(BF)
    extra = dot(x[pl.ds(ROWS, EXTRA)], g[...])
    own_vec = [extra[k : k + 1] + (extra[3 + k : 4 + k] + extra[6 + k : 7 + k]) for k in range(3)]
    own_species = extra[9:10]
    for pair in range(GROUPS):
        s = own_species[:, pair * PAIR : (pair + 1) * PAIR]
        send_s[2 * pair : 2 * pair + 1] = s
        send_s[2 * pair + 1 : 2 * pair + 2] = pltpu.roll(s, BLOCK, 1)
    for d in range(8):
        copies_s[d].start()

    loads["table"].wait()
    for j in range(4):
        for h in range(2):
            row = tab[j : j + 1, h * 128 : (h + 1) * 128]
            tb[j, pl.ds(h * 128, 128)] = jnp.broadcast_to(row, (128, 128)).T
    for name in ("reverse", "wq", "wk", "wv", "wo", "wi", "wm", "wg", "wr", "wx", "we", "wrev", "wc"):
        loads[name].wait()
    wi[...] = wit[...].astype(F32).T.astype(BF)

    weights = (wq, wkv, wo, wi, wm, wgr, wx, wer, wc)

    def columns(t):
        return pl.ds(t * TILE if isinstance(t, int) else pl.multiple_of(t * TILE, TILE), TILE)

    def gather(t, p, turned):
        p[...] = one_hot(E, 0, rev[:, columns(t)])
        turned[...] = dot(x[...], p[...]).astype(BF)

    def work(t, turned):
        cols = columns(t)
        here, there = x[pl.ds(0, C), cols], turned[pl.ds(0, C)]
        species_there = turned[pl.ds(ROWS, EXTRA)].astype(F32)[9:10]
        embedded = jnp.concatenate([embed(here, tb, spc[:, cols]), embed(there, tb, species_there)], axis=1)

        def store(k, new):
            out[pl.ds(C + k * MUL, MUL) if k >= 0 else pl.ds(0, C), cols] = new

        edge_update(
            lambda k: x[pl.ds(C + k * MUL, MUL), cols],
            lambda k: turned[pl.ds(C + k * MUL, MUL)],
            embedded,
            jnp.concatenate([there, here], axis=1),
            harmonics(vec[0, :, cols], vec[1, :, cols], vec[2, :, cols]),
            *weights,
            store,
        )

    def two_tiles(u, carry):
        gather(2 * u + 1, p1, rev1)
        work(2 * u, rev0)
        gather(2 * u + 2, p0, rev0)
        work(2 * u + 1, rev1)
        return carry

    tiles = E // TILE
    gather(0, p0, rev0)
    lax.fori_loop(0, tiles // 2 - 1, two_tiles, 0)
    gather(tiles - 1, p1, rev1)
    work(tiles - 2, rev0)
    work(tiles - 1, rev1)

    def unpack(a, b):
        a, b = a.astype(F32), b.astype(F32)
        top = jnp.where(lane < BLOCK, a, pltpu.roll(b, BLOCK, 1))
        bottom = jnp.where(lane < BLOCK, pltpu.roll(a, BLOCK, 1), b)
        return jnp.concatenate([top, bottom], axis=0).astype(BF)

    for pair in ARRIVAL:
        cols = pl.ds(pair * PAIR, PAIR)
        for d in (2 * pair, 2 * pair + 1):
            copies_a[OPPOSITE[d]].wait_recv()
            copies_s[OPPOSITE[d]].wait_recv()
        here = own[pl.ds(0, C), cols]
        there = unpack(recv_a[2 * pair], recv_a[2 * pair + 1])
        species_there = jnp.where(
            lane < BLOCK, recv_s[2 * pair : 2 * pair + 1], pltpu.roll(recv_s[2 * pair + 1 : 2 * pair + 2], BLOCK, 1)
        )
        species_both = jnp.concatenate([own_species[:, pair * PAIR : (pair + 1) * PAIR], species_there], axis=1)
        embedded = embed(jnp.concatenate([here, there], axis=1), tb, species_both)
        for d in (2 * pair, 2 * pair + 1):
            copies_b[OPPOSITE[d]].wait_recv()
        rev0[pl.ds(C, ROWS_T), pl.ds(0, PAIR)] = unpack(recv_b[2 * pair], recv_b[2 * pair + 1])

        def store(k, new):
            rows = pl.ds(C + k * MUL, MUL) if k >= 0 else pl.ds(0, C)
            y_late[rows, cols] = new

        edge_update(
            lambda k: own[pl.ds(C + k * MUL, MUL), cols],
            lambda k: rev0[pl.ds(C + k * MUL, MUL), pl.ds(0, PAIR)],
            embedded,
            jnp.concatenate([there, here], axis=1),
            harmonics(*[u[:, pair * PAIR : (pair + 1) * PAIR] for u in own_vec]),
            *weights,
            store,
        )
    for d in range(8):
        copies_a[d].wait_send()
        copies_b[d].wait_send()
        copies_s[d].wait_send()


CHUNKS = (128, 128, 192, 192, 128, 64)


def final_kernel(part, last, reverse_h, scalars_h, tensors_h, done, rev, hot, load_sem, store_sem):
    load = pltpu.make_async_copy(reverse_h, rev, load_sem)
    load.start()
    load.wait()
    slot = slot_of(rev[...])
    hot[...] = one_hot(SLOTS - EARLY, EARLY, slot)
    stores = []
    start = 0
    for i, rows in enumerate(CHUNKS):
        for t in range(0, E, 512):
            moved = dot(last[pl.ds(start, rows)], hot[:, pl.ds(t, 512)]).astype(BF)
            block = (pl.ds(start, rows), pl.ds(t, 512))
            done[block] = jnp.where(slot[:, t : t + 512] >= EARLY, moved, part[block])
        dst = scalars_h.at[pl.ds(start, rows)] if start < C else tensors_h.at[pl.ds(start - C, rows)]
        copy = pltpu.make_async_copy(done.at[pl.ds(start, rows)], dst, store_sem.at[i])
        copy.start()
        stores.append(copy)
        start += rows
    for copy in stores:
        copy.wait()


def per_device(
    nx, ny,
    scalars, tensors, vectors, species, species_table, reverse, send_index, counts,
    w_query, w_key, w_value, w_output, w_invariant, w_message, w_gate, w_radial, w_mixing, w_expand, w_reverse, w_contract,
):
    reverse_row = reverse.reshape(1, E)
    hbm = pl.BlockSpec(memory_space=pltpu.HBM)
    vmem = pl.BlockSpec(memory_space=pltpu.VMEM)
    part, last = pl.pallas_call(
        functools.partial(exchange_kernel, nx, ny),
        out_shape=(pltpu.VMEM((ROWS, E), BF), pltpu.VMEM((ROWS, SLOTS - EARLY), BF)),
        in_specs=[hbm] * 19,
        out_specs=(vmem, vmem),
        scratch_shapes=[
            pltpu.VMEM((ROWS + EXTRA, E), BF),
            pltpu.VMEM((3, 1, E), F32),
            pltpu.VMEM((1, E), jnp.int32),
            pltpu.VMEM((4, C), F32),
            pltpu.VMEM((1, E), jnp.int32),
            pltpu.VMEM((8, BLOCK), jnp.int32),
            pltpu.VMEM((C, C), BF),
            pltpu.VMEM((2 * C, C), BF),
            pltpu.VMEM((C, C), BF),
            pltpu.VMEM((3 * MUL, C), BF),
            pltpu.VMEM((C, 3 * MUL), BF),
            pltpu.VMEM((C, C), BF),
            pltpu.VMEM((6 * MUL, C), BF),
            pltpu.VMEM((MUL, MUL), BF),
            pltpu.VMEM((FFN, 2 * C), BF),
            pltpu.VMEM((C, FFN), BF),
            pltpu.VMEM((E, SLOTS), BF),
            pltpu.VMEM((E, TILE), BF),
            pltpu.VMEM((E, TILE), BF),
            pltpu.VMEM((ROWS + EXTRA, TILE), BF),
            pltpu.VMEM((ROWS + EXTRA, TILE), BF),
            pltpu.VMEM((ROWS, SLOTS), BF),
            pltpu.VMEM((8, C // 2, 128), BF),
            pltpu.VMEM((8, ROWS_T // 2, 128), BF),
            pltpu.VMEM((8, C // 2, 128), BF),
            pltpu.VMEM((8, ROWS_T // 2, 128), BF),
            pltpu.VMEM((8, 128), F32),
            pltpu.VMEM((8, 128), F32),
            pltpu.VMEM((4, C, 128), F32),
            pltpu.SemaphoreType.DMA((19,)),
            pltpu.SemaphoreType.DMA((3, 8)),
            pltpu.SemaphoreType.DMA((3, 8)),
        ],
        compiler_params=pltpu.CompilerParams(collective_id=0, has_side_effects=True, vmem_limit_bytes=59 * 2**20),
        cost_estimate=pl.CostEstimate(flops=16 * 10**9, bytes_accessed=9 * 2**20, transcendentals=3 * 10**6),
        name="exchange",
    )(
        scalars.reshape(C, E), tensors.reshape(ROWS_T, E), vectors.reshape(3, 1, E), species.reshape(1, E),
        species_table.T, reverse_row, send_index.reshape(8, BLOCK),
        w_query, w_key, w_value, w_output, w_invariant.T, w_message, w_gate, w_radial, w_mixing,
        w_expand, w_reverse, w_contract,
    )
    new_scalars, new_tensors = pl.pallas_call(
        final_kernel,
        out_shape=(jax.ShapeDtypeStruct((C, E), BF), jax.ShapeDtypeStruct((ROWS_T, E), BF)),
        in_specs=[vmem, vmem, hbm],
        out_specs=(hbm, hbm),
        scratch_shapes=[
            pltpu.VMEM((ROWS, E), BF),
            pltpu.VMEM((1, E), jnp.int32),
            pltpu.VMEM((SLOTS - EARLY, E), BF),
            pltpu.SemaphoreType.DMA,
            pltpu.SemaphoreType.DMA((len(CHUNKS),)),
        ],
        compiler_params=pltpu.CompilerParams(vmem_limit_bytes=24 * 2**20),
        cost_estimate=pl.CostEstimate(flops=10**9, bytes_accessed=7 * 2**20, transcendentals=0),
        name="combine",
    )(part, last, reverse_row)
    return new_scalars.reshape(1, 1, C, E), new_tensors.reshape(1, 1, 9, MUL, E)


def solution(mesh):
    split = P("gx", "gy")
    return jax.shard_map(
        functools.partial(per_device, mesh.shape["gx"], mesh.shape["gy"]),
        mesh=mesh,
        in_specs=(split,) * 4 + (P(),) + (split,) * 3 + (P(),) * 12,
        out_specs=(split, split),
        check_vma=False,
    )
```
